32 devices in a mesh: grp: 2 (over x), blk: 16 (over z, y, core).
Axes of the slice: x: 2, y: 2, z: 4, core: 2. Of those that a mesh axis runs over, the one named last changes fastest.
Arguments:
- vertex_embed: float32 [12288, 256], P(('grp', 'blk')), may hold values from -1.8 to 1.8
- context_embed: float32 [12288, 256], P(('grp', 'blk')), may hold values from -1.8 to 1.8
- counts: int32 [4, 12288, 384], P(None, ('grp', 'blk')), may hold values from 0 to 7
- negatives: int32 [4, 5, 12288], P(None, None, ('grp', 'blk')), may hold values from 0 to 383
- masks: int32 [4, 96, 3], P(None, ('grp', 'blk')), may hold values 0 or 1
Outputs:
- vertex_final: float32 [12288, 256], P(('grp', 'blk'))
- context_final: float32 [12288, 256], P(('grp', 'blk'))
The draws below stay inside these ranges and needn't reach their ends.
All inputs are finite; a program needn't handle non-finite values. No bound on the sum of `masks` on one device may be relied on, other than what follows from the above.
Results may differ from the reference program's by a relative error of at most 0.0003.
Values sent between devices are 32-bit elements; how exact they have to be, the bound alone decides.
A program may use at most 64 MiB of HBM per device.

```python
import math
import jax
import jax.numpy as jnp
from jax import lax

W = 256
ROWS = 384
TILE = 128
NEGS = 5
ROUNDS = 2
ROUND_PASSES = 2
PASSES = 4
TILES = 3
VERTS = 12288
N_GRP = 2
N_BLK = 16
DEVICES = 32


def plant(drawn, stream_key, least, largest):
    extent = drawn.shape
    spot = [jax.random.randint(jax.random.fold_in(stream_key, axis), (), 0, extent[axis]) for axis in range(len(extent))]
    drawn = drawn.at[tuple(spot)].set(least)
    longest = extent.index(max(extent))
    spot[longest] = (spot[longest] + 1) % extent[longest]
    return drawn.at[tuple(spot)].set(largest)


def steps_of(stream_key, extent, pieces, low, largest):
    def one(dim, blocks):
        steps = jax.random.uniform(jax.random.fold_in(jax.random.fold_in(stream_key, 6), dim), (blocks,), jnp.float32, low / len(pieces), largest / len(pieces))
        return jnp.repeat(jnp.exp(steps), extent[dim] // blocks).reshape((-1,) + (1,) * (len(extent) - dim - 1))

    factor_of = one(*pieces[0])
    for cut in pieces[1:]:
        factor_of = factor_of * one(*cut)
    return factor_of


def normal_values(key, extent, width, limit, shards=(), kind=jnp.bfloat16):
    factor_of = steps_of(key, extent, shards, -0.22, 0.18) if shards else 1.0
    array = jax.random.normal(key, extent, jnp.float32) * width * factor_of
    return jnp.minimum(jnp.maximum(array, -limit), limit).astype(kind)


def setup_inputs(seed: int = 0) -> dict:
    key_of = jax.random.split(jax.random.key(seed), 6)
    return {
        "vertex_embed": normal_values(key_of[0], (VERTS, W), 0.3, 1.8, ((0, 32),), jnp.float32),
        "context_embed": normal_values(key_of[1], (VERTS, W), 0.3, 1.8, ((0, 32),), jnp.float32),
        "counts": plant(jax.random.randint(key_of[2], (PASSES, VERTS, ROWS), 0, 8), jax.random.fold_in(key_of[2], 1), 0, 7).astype(jnp.int32),
        "negatives": plant(jax.random.randint(key_of[3], (PASSES, NEGS, VERTS), 0, ROWS), jax.random.fold_in(key_of[3], 1), 0, ROWS - 1).astype(jnp.int32),
        "masks": plant((jax.random.randint(key_of[4], (PASSES, DEVICES * TILES, TILES), 0, 4) < 3).astype(jnp.int32), jax.random.fold_in(key_of[4], 1), 0, 1),
    }


def reference(vertex_embed, context_embed, counts, negatives, masks):
    highest = lax.Precision.HIGHEST
    vert = vertex_embed.reshape(N_GRP, N_BLK, ROWS, W)
    ctx = context_embed.reshape(N_GRP, N_BLK, ROWS, W)
    cnt = counts.reshape(PASSES, N_GRP, N_BLK, ROWS, ROWS)
    neg = negatives.reshape(PASSES, NEGS, N_GRP, N_BLK, ROWS)
    msk = masks.reshape(PASSES, N_GRP, N_BLK, TILES, TILES)
    columns = jnp.arange(ROWS, dtype=jnp.int32)
    eta = 0.25 / math.sqrt(ROWS)
    for rnd in range(ROUNDS):
        if rnd > 0:
            vert = jnp.flip(vert.reshape(N_GRP // 2, 2, N_BLK, ROWS, W), axis=1).reshape(N_GRP, N_BLK, ROWS, W)
        for step in range(ROUND_PASSES):
            index = rnd * ROUND_PASSES + step
            scores = jnp.einsum('gbiw,gbjw->gbij', vert, ctx, precision=highest)
            sig = jax.nn.sigmoid(scores)
            negcount = jnp.zeros((N_GRP, N_BLK, ROWS, ROWS), jnp.float32)
            for sample in range(NEGS):
                negcount = negcount + (neg[index, sample][..., :, None] == columns).astype(jnp.float32)
            coef = cnt[index].astype(jnp.float32) * (1.0 - sig) - negcount * sig
            gate = msk[index].astype(jnp.float32)[:, :, :, None, :, None]
            coef = (coef.reshape(N_GRP, N_BLK, TILES, TILE, TILES, TILE) * gate).reshape(N_GRP, N_BLK, ROWS, ROWS)
            new_vert = vert + eta * jnp.einsum('gbij,gbjw->gbiw', coef, ctx, precision=highest)
            new_ctx = ctx + eta * jnp.einsum('gbij,gbiw->gbjw', coef, vert, precision=highest)
            vert = new_vert
            ctx = jnp.roll(new_ctx, 1, axis=1)
    return (vert.reshape(VERTS, W), ctx.reshape(VERTS, W))
```

```python
import functools
import math

import jax
import jax.numpy as jnp
from jax import lax
from jax.experimental import pallas as pl
from jax.experimental.pallas import tpu as pltpu
from jax.sharding import PartitionSpec as P

ROUNDS = 2
ROUND_PASSES = 2
PASSES = ROUNDS * ROUND_PASSES
F32 = jnp.float32
BF16 = jnp.bfloat16
MESH = pl.DeviceIdType.MESH


def halves(x):
    hi = x.astype(BF16)
    return hi, (x - hi.astype(F32)).astype(BF16)


def dot3(a, b, dims):
    def one(x, y):
        return lax.dot_general(x, y, (dims, ((), ())), preferred_element_type=F32)

    return one(a[0], b[0]) + (one(a[0], b[1]) + one(a[1], b[0]))


NN = ((1,), (0,))
NT = ((1,), (1,))
TN = ((0,), (0,))


def kernel(
    tiles, v_hbm, c_hbm, cnt_hbm, neg_ref, mask_ref, vout, cout,
    vbuf, cbuf, cnt, pbuf, qbuf, vsplit, csplit,
    in_sem, cnt_sem, csend, crecv, vsend, vrecv,
):
    rows = v_hbm.shape[0]
    tile = rows // tiles
    eta = 0.25 / math.sqrt(rows)
    negs = neg_ref.shape[1]
    grp, blk = lax.axis_index("grp"), lax.axis_index("blk")
    n = lax.axis_size("blk")
    right = (grp, lax.rem(blk + 1, n))
    left = (grp, lax.rem(blk + n - 1, n))
    partner = (grp + 1 - 2 * lax.rem(grp, 2), blk)

    barrier = pltpu.get_barrier_semaphore()
    for other in (left, partner):
        pl.semaphore_signal(barrier, inc=1, device_id=other, device_id_type=MESH)

    load_cnt = [pltpu.make_async_copy(cnt_hbm.at[q], cnt.at[q], cnt_sem.at[q]) for q in range(PASSES)]
    load_v = pltpu.make_async_copy(v_hbm, vbuf.at[0], in_sem.at[0])
    load_c = pltpu.make_async_copy(c_hbm, cbuf.at[0], in_sem.at[1])
    load_cnt[0].start()
    load_v.start()
    load_c.start()
    for q in range(1, PASSES):
        load_cnt[q].start()

    def span(k):
        return pl.ds(k * tile, tile)

    def prepare(q):
        load_cnt[q].wait()
        picked = neg_ref[q].astype(F32)
        picked = jnp.concatenate([picked, jnp.full((8 - negs % 8, rows), -1.0, F32)], axis=0).T
        for i in range(tiles):
            mine = picked[i * tile : (i + 1) * tile]
            for j in range(tiles):
                columns = (lax.broadcasted_iota(jnp.int32, (tile, tile), 1) + j * tile).astype(F32)
                seen = jnp.zeros((tile, tile), F32)
                for s in range(negs):
                    seen = seen + jnp.where(mine[:, s : s + 1] == columns, 1.0, 0.0)
                scale = mask_ref[q, i, j].astype(F32) * (0.5 * eta)
                pos = cnt[q, span(i), span(j)].astype(F32)
                pbuf[q, span(i), span(j)] = (pos - seen) * scale
                qbuf[q, span(i), span(j)] = (pos + seen) * scale

    def c_copy(q, k):
        target = cbuf.at[q + 1] if q < PASSES - 1 else cout
        source = cnew(q).at[span(k)]
        return pltpu.make_async_remote_copy(
            src_ref=source, dst_ref=target.at[span(k)], send_sem=csend.at[q, k],
            recv_sem=crecv.at[q, k], device_id=right, device_id_type=MESH,
        )

    def cnew(q):
        return cbuf.at[PASSES + q]

    def v_copy(k):
        return pltpu.make_async_remote_copy(
            src_ref=vbuf.at[2, span(k)], dst_ref=vbuf.at[3, span(k)], send_sem=vsend.at[k],
            recv_sem=vrecv.at[k], device_id=partner, device_id_type=MESH,
        )

    def by_context(q, vin, vnext):
        vhi, vlo = halves(vin[...])
        vsplit[0] = vhi
        vsplit[1] = vlo
        for j in range(tiles):
            if q > 0:
                c_copy(q - 1, j).wait_recv()
            ctx = cbuf[q, span(j)]
            chl = halves(ctx)
            vhl = (vsplit[0], vsplit[1])
            scores = dot3(vhl, chl, NT)
            coef = halves(pbuf[q, :, span(j)] - qbuf[q, :, span(j)] * jnp.tanh(0.5 * scores))
            cnew(q)[span(j)] = ctx + dot3(coef, vhl, TN)
            if q == 0 and j == 0:
                pl.semaphore_wait(barrier, 2)
            c_copy(q, j).start()
            base = vin[...] if j == 0 else vnext[...]
            vnext[...] = base + dot3(coef, chl, NN)

    def by_vertex(q, vin, vnext):
        for j in range(tiles):
            c_copy(q - 1, j).wait_recv()
        chi, clo = halves(cbuf[q])
        csplit[0] = chi
        csplit[1] = clo
        for i in range(tiles):
            v_copy(i).wait_recv()
            vert = vin[span(i)]
            vhl = halves(vert)
            chl = (csplit[0], csplit[1])
            scores = dot3(vhl, chl, NT)
            coef = halves(pbuf[q, span(i)] - qbuf[q, span(i)] * jnp.tanh(0.5 * scores))
            base = cbuf[q] if i == 0 else cnew(q)[...]
            cnew(q)[...] = base + dot3(coef, vhl, TN)
            if i == tiles - 1:
                for j in range(tiles):
                    c_copy(q, j).start()
            vnext[span(i)] = vert + dot3(coef, chl, NN)

    prepare(0)
    load_v.wait()
    load_c.wait()
    by_context(0, vbuf.at[0], vbuf.at[1])
    prepare(1)
    by_context(1, vbuf.at[1], vbuf.at[2])
    for k in range(tiles):
        v_copy(k).start()
    prepare(2)
    prepare(3)
    by_vertex(2, vbuf.at[3], vbuf.at[4])
    by_context(3, vbuf.at[4], vout)
    for j in range(tiles):
        c_copy(PASSES - 1, j).wait_recv()
    for k in range(tiles):
        v_copy(k).wait_send()
        for q in range(PASSES):
            c_copy(q, k).wait_send()


def on_device(vertex_embed, context_embed, counts, negatives, masks):
    rows, width = vertex_embed.shape
    tiles = masks.shape[1]
    state = jax.ShapeDtypeStruct((rows, width), F32)
    hbm = pl.BlockSpec(memory_space=pl.ANY)
    vmem = pl.BlockSpec(memory_space=pltpu.VMEM)
    return pl.pallas_call(
        functools.partial(kernel, tiles),
        out_shape=(state, state),
        in_specs=[hbm, hbm, hbm, vmem, pl.BlockSpec(memory_space=pltpu.SMEM)],
        out_specs=(vmem, vmem),
        scratch_shapes=[
            pltpu.VMEM((5, rows, width), F32),
            pltpu.VMEM((2 * PASSES, rows, width), F32),
            pltpu.VMEM((PASSES, rows, rows), jnp.int32),
            pltpu.VMEM((PASSES, rows, rows), F32),
            pltpu.VMEM((PASSES, rows, rows), F32),
            pltpu.VMEM((2, rows, width), BF16),
            pltpu.VMEM((2, rows, width), BF16),
            pltpu.SemaphoreType.DMA((2,)),
            pltpu.SemaphoreType.DMA((PASSES,)),
            pltpu.SemaphoreType.DMA((PASSES, tiles)),
            pltpu.SemaphoreType.DMA((PASSES, tiles)),
            pltpu.SemaphoreType.DMA((tiles,)),
            pltpu.SemaphoreType.DMA((tiles,)),
        ],
        compiler_params=pltpu.CompilerParams(
            collective_id=0, has_side_effects=True, vmem_limit_bytes=40 * 1024 * 1024
        ),
    )(vertex_embed, context_embed, counts, negatives, masks)


def solution(mesh):
    placed = (
        P(("grp", "blk"), None),
        P(("grp", "blk"), None),
        P(None, ("grp", "blk"), None),
        P(None, None, ("grp", "blk")),
        P(None, ("grp", "blk"), None),
    )
    return jax.shard_map(
        on_device,
        mesh=mesh,
        in_specs=placed,
        out_specs=(P(("grp", "blk"), None), P(("grp", "blk"), None)),
        check_vma=False,
    )
```

```python
import functools
import math

import jax
import jax.numpy as jnp
from jax import lax
from jax.experimental import pallas as pl
from jax.experimental.pallas import tpu as pltpu
from jax.sharding import PartitionSpec as P

ROUNDS = 2
ROUND_PASSES = 2
PASSES = ROUNDS * ROUND_PASSES
F32 = jnp.float32
BF16 = jnp.bfloat16
MESH = pl.DeviceIdType.MESH


def halves(x):
    hi = x.astype(BF16)
    return hi, (x - hi.astype(F32)).astype(BF16)


def dot3(a, b, dims):
    left, right = dims[0][0], dims[1][0]
    stacked_a = jnp.concatenate([a[0], a[0], a[1]], axis=left)
    stacked_b = jnp.concatenate([b[0], b[1], b[0]], axis=right)
    return lax.dot_general(stacked_a, stacked_b, (dims, ((), ())), preferred_element_type=F32)


NN = ((1,), (0,))
NT = ((1,), (1,))
TN = ((0,), (0,))


def kernel(
    tiles, v_hbm, c_hbm, cnt_hbm, neg_ref, mask_ref, vout, cout,
    vbuf, cbuf, cnt, pbuf, qbuf, vsplit, csplit,
    in_sem, cnt_sem, csend, crecv, vsend, vrecv,
):
    rows = v_hbm.shape[0]
    tile = rows // tiles
    eta = 0.25 / math.sqrt(rows)
    negs = neg_ref.shape[0]
    grp, blk = lax.axis_index("grp"), lax.axis_index("blk")
    n = lax.axis_size("blk")
    right = (grp, lax.rem(blk + 1, n))
    left = (grp, lax.rem(blk + n - 1, n))
    partner = (grp + 1 - 2 * lax.rem(grp, 2), blk)

    barrier = pltpu.get_barrier_semaphore()
    for other in (left, partner):
        pl.semaphore_signal(barrier, inc=1, device_id=other, device_id_type=MESH)

    load_cnt = [pltpu.make_async_copy(cnt_hbm.at[q], cnt.at[q], cnt_sem.at[q]) for q in range(PASSES)]
    load_v = pltpu.make_async_copy(v_hbm, vbuf.at[0], in_sem.at[0])
    load_c = pltpu.make_async_copy(c_hbm, cbuf.at[0], in_sem.at[1])
    load_cnt[0].start()
    load_v.start()
    load_c.start()

    def span(k):
        return pl.ds(k * tile, tile)

    def prepare_by_context(q):
        load_cnt[q].wait()
        for j in range(tiles):
            column = lax.broadcasted_iota(jnp.int32, (tile, rows), 0) + j * tile
            seen = jnp.zeros((tile, rows), F32)
            for s in range(negs):
                seen = seen + jnp.where(neg_ref[s, q : q + 1, :] == column, 1.0, 0.0)
            for i in range(tiles):
                scale = mask_ref[i, q, j].astype(F32) * (0.5 * eta)
                pos = cnt[q, span(i), span(j)].astype(F32).T
                there = seen[:, i * tile : (i + 1) * tile]
                pbuf[q, span(j), span(i)] = (pos - there) * scale
                qbuf[q, span(j), span(i)] = (pos + there) * scale

    def prepare_by_vertex(q):
        load_cnt[q].wait()
        picked = neg_ref[:, q, :].astype(F32)
        picked = jnp.concatenate([picked, jnp.full((8 - negs % 8, rows), -1.0, F32)], axis=0).T
        for i in range(tiles):
            mine = picked[i * tile : (i + 1) * tile]
            for j in range(tiles):
                columns = (lax.broadcasted_iota(jnp.int32, (tile, tile), 1) + j * tile).astype(F32)
                seen = jnp.zeros((tile, tile), F32)
                for s in range(negs):
                    seen = seen + jnp.where(mine[:, s : s + 1] == columns, 1.0, 0.0)
                scale = mask_ref[i, q, j].astype(F32) * (0.5 * eta)
                pos = cnt[q, span(i), span(j)].astype(F32)
                pbuf[q, span(i), span(j)] = (pos - seen) * scale
                qbuf[q, span(i), span(j)] = (pos + seen) * scale

    def c_copy(q, k):
        target = cbuf.at[q + 1] if q < PASSES - 1 else cout
        source = cnew(q).at[span(k)]
        return pltpu.make_async_remote_copy(
            src_ref=source, dst_ref=target.at[span(k)], send_sem=csend.at[q, k],
            recv_sem=crecv.at[q, k], device_id=right, device_id_type=MESH,
        )

    def cnew(q):
        return cbuf.at[PASSES + q]

    def v_copy(k):
        return pltpu.make_async_remote_copy(
            src_ref=vbuf.at[2, span(k)], dst_ref=vbuf.at[3, span(k)], send_sem=vsend.at[k],
            recv_sem=vrecv.at[k], device_id=partner, device_id_type=MESH,
        )

    def by_context(q, vin, vnext):
        vhi, vlo = halves(vin[...])
        vsplit[0] = vhi
        vsplit[1] = vlo
        for j in range(tiles):
            if q > 0:
                c_copy(q - 1, j).wait_recv()
            ctx = cbuf[q, span(j)]
            chl = halves(ctx)
            vhl = (vsplit[0], vsplit[1])
            scores = dot3(chl, vhl, NT)
            coef = halves(pbuf[q, span(j)] - qbuf[q, span(j)] * jnp.tanh(0.5 * scores))
            cnew(q)[span(j)] = ctx + dot3(coef, vhl, NN)
            if q == 0 and j == 0:
                pl.semaphore_wait(barrier, 2)
            c_copy(q, j).start()
            base = vin[...] if j == 0 else vnext[...]
            vnext[...] = base + dot3(coef, chl, TN)

    def by_vertex(q, vin, vnext):
        for j in range(tiles):
            c_copy(q - 1, j).wait_recv()
        chi, clo = halves(cbuf[q])
        csplit[0] = chi
        csplit[1] = clo
        for i in range(tiles):
            v_copy(i).wait_recv()
            vert = vin[span(i)]
            vhl = halves(vert)
            chl = (csplit[0], csplit[1])
            scores = dot3(vhl, chl, NT)
            coef = halves(pbuf[q, span(i)] - qbuf[q, span(i)] * jnp.tanh(0.5 * scores))
            base = cbuf[q] if i == 0 else cnew(q)[...]
            cnew(q)[...] = base + dot3(coef, vhl, TN)
            if i == tiles - 1:
                for j in range(tiles):
                    c_copy(q, j).start()
            vnext[span(i)] = vert + dot3(coef, chl, NN)

    prepare_by_context(0)
    load_v.wait()
    load_c.wait()
    for q in range(1, PASSES):
        load_cnt[q].start()
    by_context(0, vbuf.at[0], vbuf.at[1])
    prepare_by_context(1)
    by_context(1, vbuf.at[1], vbuf.at[2])
    for k in range(tiles):
        v_copy(k).start()
    prepare_by_vertex(2)
    prepare_by_context(3)
    by_vertex(2, vbuf.at[3], vbuf.at[4])
    by_context(3, vbuf.at[4], vout)
    for j in range(tiles):
        c_copy(PASSES - 1, j).wait_recv()
    for k in range(tiles):
        v_copy(k).wait_send()
        for q in range(PASSES):
            c_copy(q, k).wait_send()


def on_device(vertex_embed, context_embed, counts, negatives, masks):
    rows, width = vertex_embed.shape
    tiles = masks.shape[1]
    state = jax.ShapeDtypeStruct((rows, width), F32)
    hbm = pl.BlockSpec(memory_space=pltpu.HBM)
    vmem = pl.BlockSpec(memory_space=pltpu.VMEM)
    return pl.pallas_call(
        functools.partial(kernel, tiles),
        out_shape=(state, state),
        in_specs=[hbm, hbm, hbm, vmem, pl.BlockSpec(memory_space=pltpu.SMEM)],
        out_specs=(vmem, vmem),
        scratch_shapes=[
            pltpu.VMEM((5, rows, width), F32),
            pltpu.VMEM((2 * PASSES, rows, width), F32),
            pltpu.VMEM((PASSES, rows, rows), jnp.int32),
            pltpu.VMEM((PASSES, rows, rows), F32),
            pltpu.VMEM((PASSES, rows, rows), F32),
            pltpu.VMEM((2, rows, width), BF16),
            pltpu.VMEM((2, rows, width), BF16),
            pltpu.SemaphoreType.DMA((2,)),
            pltpu.SemaphoreType.DMA((PASSES,)),
            pltpu.SemaphoreType.DMA((PASSES, tiles)),
            pltpu.SemaphoreType.DMA((PASSES, tiles)),
            pltpu.SemaphoreType.DMA((tiles,)),
            pltpu.SemaphoreType.DMA((tiles,)),
        ],
        compiler_params=pltpu.CompilerParams(
            collective_id=0, has_side_effects=True, vmem_limit_bytes=60 * 1024 * 1024
        ),
    )(vertex_embed, context_embed, counts, negatives.transpose(1, 0, 2), masks.transpose(1, 0, 2))


def solution(mesh):
    placed = (
        P(("grp", "blk"), None),
        P(("grp", "blk"), None),
        P(None, ("grp", "blk"), None),
        P(None, None, ("grp", "blk")),
        P(None, ("grp", "blk"), None),
    )
    return jax.shard_map(
        on_device,
        mesh=mesh,
        in_specs=placed,
        out_specs=(P(("grp", "blk"), None), P(("grp", "blk"), None)),
        check_vma=False,
    )
```

```python
import functools
import math

import jax
import jax.numpy as jnp
from jax import lax
from jax.experimental import pallas as pl
from jax.experimental.pallas import tpu as pltpu
from jax.sharding import PartitionSpec as P

ROUNDS = 2
ROUND_PASSES = 2
PASSES = ROUNDS * ROUND_PASSES
F32 = jnp.float32
BF16 = jnp.bfloat16
MESH = pl.DeviceIdType.MESH


def halves(x):
    hi = x.astype(BF16)
    return hi, (x - hi.astype(F32)).astype(BF16)


def dot3(a, b, dims):
    left, right = dims[0][0], dims[1][0]
    stacked_a = jnp.concatenate([a[0], a[0], a[1]], axis=left)
    stacked_b = jnp.concatenate([b[0], b[1], b[0]], axis=right)
    return lax.dot_general(stacked_a, stacked_b, (dims, ((), ())), preferred_element_type=F32)


NN = ((1,), (0,))
NT = ((1,), (1,))
TN = ((0,), (0,))


def kernel(
    tiles, v_hbm, c_hbm, cnt_hbm, neg_ref, mask_ref, vout, cout,
    vbuf, cbuf, cnt, pbuf, qbuf, vsplit, csplit,
    in_sem, cnt_sem, csend, crecv, vsend, vrecv,
):
    rows = v_hbm.shape[0]
    tile = rows // tiles
    eta = 0.25 / math.sqrt(rows)
    negs = neg_ref.shape[0]
    grp, blk = lax.axis_index("grp"), lax.axis_index("blk")
    n = lax.axis_size("blk")
    right = (grp, lax.rem(blk + 1, n))
    left = (grp, lax.rem(blk + n - 1, n))
    partner = (grp + 1 - 2 * lax.rem(grp, 2), blk)

    barrier = pltpu.get_barrier_semaphore()
    for other in (left, partner):
        pl.semaphore_signal(barrier, inc=1, device_id=other, device_id_type=MESH)

    load_cnt = [pltpu.make_async_copy(cnt_hbm.at[q], cnt.at[q], cnt_sem.at[q]) for q in range(PASSES)]
    load_v = pltpu.make_async_copy(v_hbm, vbuf.at[0], in_sem.at[0])
    load_c = pltpu.make_async_copy(c_hbm, cbuf.at[0], in_sem.at[1])
    load_cnt[0].start()
    load_v.start()
    load_c.start()

    def span(k):
        return pl.ds(k * tile, tile)

    def prepare_by_context(q):
        load_cnt[q].wait()
        for j in range(tiles):
            column = lax.broadcasted_iota(jnp.int32, (tile, rows), 0) + j * tile
            seen = jnp.zeros((tile, rows), F32)
            for s in range(negs):
                seen = seen + jnp.where(neg_ref[s, q : q + 1, :] == column, 1.0, 0.0)
            for i in range(tiles):
                scale = mask_ref[i, q, j].astype(F32) * (0.5 * eta)
                pos = cnt[q, span(i), span(j)].astype(F32).T
                there = seen[:, i * tile : (i + 1) * tile]
                pbuf[q, span(j), span(i)] = (pos - there) * scale
                qbuf[q, span(j), span(i)] = (pos + there) * scale

    def prepare_by_vertex(q):
        load_cnt[q].wait()
        picked = neg_ref[:, q, :].astype(F32)
        picked = jnp.concatenate([picked, jnp.full((8 - negs % 8, rows), -1.0, F32)], axis=0).T
        for i in range(tiles):
            mine = picked[i * tile : (i + 1) * tile]
            for j in range(tiles):
                columns = (lax.broadcasted_iota(jnp.int32, (tile, tile), 1) + j * tile).astype(F32)
                seen = jnp.zeros((tile, tile), F32)
                for s in range(negs):
                    seen = seen + jnp.where(mine[:, s : s + 1] == columns, 1.0, 0.0)
                scale = mask_ref[i, q, j].astype(F32) * (0.5 * eta)
                pos = cnt[q, span(i), span(j)].astype(F32)
                pbuf[q, span(i), span(j)] = (pos - seen) * scale
                qbuf[q, span(i), span(j)] = (pos + seen) * scale

    def c_copy(q, k):
        target = cbuf.at[q + 1] if q < PASSES - 1 else cout
        source = cnew(q).at[span(k)]
        return pltpu.make_async_remote_copy(
            src_ref=source, dst_ref=target.at[span(k)], send_sem=csend.at[q, k],
            recv_sem=crecv.at[q, k], device_id=right, device_id_type=MESH,
        )

    def cnew(q):
        return cbuf.at[PASSES + q]

    def v_copy(k):
        return pltpu.make_async_remote_copy(
            src_ref=vbuf.at[2, span(k)], dst_ref=vbuf.at[3, span(k)], send_sem=vsend.at[k],
            recv_sem=vrecv.at[k], device_id=partner, device_id_type=MESH,
        )

    def by_context(q, vin, vnext):
        vhi, vlo = halves(vin[...])
        vsplit[0] = vhi
        vsplit[1] = vlo
        for j in range(tiles):
            if q > 0:
                c_copy(q - 1, j).wait_recv()
            ctx = cbuf[q, span(j)]
            chl = halves(ctx)
            vhl = (vsplit[0], vsplit[1])
            scores = dot3(chl, vhl, NT)
            coef = halves(pbuf[q, span(j)] - qbuf[q, span(j)] * jnp.tanh(0.5 * scores))
            cnew(q)[span(j)] = ctx + dot3(coef, vhl, NN)
            if q == 0 and j == 0:
                pl.semaphore_wait(barrier, 2)
            c_copy(q, j).start()
            base = vin[...] if j == 0 else vnext[...]
            vnext[...] = base + dot3(coef, chl, TN)

    def by_vertex(q, vin, vnext):
        for j in range(tiles):
            c_copy(q - 1, j).wait_recv()
        chi, clo = halves(cbuf[q])
        csplit[0] = chi
        csplit[1] = clo
        for i in range(tiles):
            if q == ROUND_PASSES:
                v_copy(i).wait_recv()
            vert = vin[span(i)]
            vhl = halves(vert)
            chl = (csplit[0], csplit[1])
            scores = dot3(vhl, chl, NT)
            coef = halves(pbuf[q, span(i)] - qbuf[q, span(i)] * jnp.tanh(0.5 * scores))
            if q == ROUND_PASSES - 1:
                vnext[span(i)] = vert + dot3(coef, chl, NN)
                v_copy(i).start()
            base = cbuf[q] if i == 0 else cnew(q)[...]
            cnew(q)[...] = base + dot3(coef, vhl, TN)
            if i == tiles - 1:
                for j in range(tiles):
                    c_copy(q, j).start()
            if q != ROUND_PASSES - 1:
                vnext[span(i)] = vert + dot3(coef, chl, NN)

    prepare_by_context(0)
    load_v.wait()
    load_c.wait()
    for q in range(1, PASSES):
        load_cnt[q].start()
    by_context(0, vbuf.at[0], vbuf.at[1])
    prepare_by_vertex(1)
    by_vertex(1, vbuf.at[1], vbuf.at[2])
    prepare_by_vertex(2)
    prepare_by_context(3)
    by_vertex(2, vbuf.at[3], vbuf.at[4])
    by_context(3, vbuf.at[4], vbuf.at[5])
    store_v = pltpu.make_async_copy(vbuf.at[5], vout, in_sem.at[0])
    store_v.start()
    for j in range(tiles):
        c_copy(PASSES - 1, j).wait_recv()
    store_v.wait()
    for k in range(tiles):
        v_copy(k).wait_send()
        for q in range(PASSES):
            c_copy(q, k).wait_send()


def on_device(vertex_embed, context_embed, counts, negatives, masks):
    rows, width = vertex_embed.shape
    tiles = masks.shape[1]
    state = jax.ShapeDtypeStruct((rows, width), F32)
    hbm = pl.BlockSpec(memory_space=pltpu.HBM)
    vmem = pl.BlockSpec(memory_space=pltpu.VMEM)
    return pl.pallas_call(
        functools.partial(kernel, tiles),
        out_shape=(state, state),
        in_specs=[hbm, hbm, hbm, vmem, pl.BlockSpec(memory_space=pltpu.SMEM)],
        out_specs=(hbm, hbm),
        scratch_shapes=[
            pltpu.VMEM((6, rows, width), F32),
            pltpu.VMEM((2 * PASSES, rows, width), F32),
            pltpu.VMEM((PASSES, rows, rows), jnp.int32),
            pltpu.VMEM((PASSES, rows, rows), F32),
            pltpu.VMEM((PASSES, rows, rows), F32),
            pltpu.VMEM((2, rows, width), BF16),
            pltpu.VMEM((2, rows, width), BF16),
            pltpu.SemaphoreType.DMA((2,)),
            pltpu.SemaphoreType.DMA((PASSES,)),
            pltpu.SemaphoreType.DMA((PASSES, tiles)),
            pltpu.SemaphoreType.DMA((PASSES, tiles)),
            pltpu.SemaphoreType.DMA((tiles,)),
            pltpu.SemaphoreType.DMA((tiles,)),
        ],
        compiler_params=pltpu.CompilerParams(
            collective_id=0, has_side_effects=True, vmem_limit_bytes=60 * 1024 * 1024
        ),
    )(vertex_embed, context_embed, counts, negatives.transpose(1, 0, 2), masks.transpose(1, 0, 2))


def solution(mesh):
    placed = (
        P(("grp", "blk"), None),
        P(("grp", "blk"), None),
        P(None, ("grp", "blk"), None),
        P(None, None, ("grp", "blk")),
        P(None, ("grp", "blk"), None),
    )
    return jax.shard_map(
        on_device,
        mesh=mesh,
        in_specs=placed,
        out_specs=(P(("grp", "blk"), None), P(("grp", "blk"), None)),
        check_vma=False,
    )
```
